512 devices in a mesh: row: 32 (over x, y, core), col: 16 (over z).
Axes of the slice: x: 4, y: 4, z: 16, core: 2. Of those that a mesh axis runs over, the one named last changes fastest.
Arguments:
- panel: bfloat16 [4, 32, 512, 512], P(None, 'row', 'col'), may hold values from -1.25 to 1.25
- diagonal_tile: float32 [512, 512], P('row', 'col'), may hold values from 0 to 2.5, as said below
- trailing: bfloat16 [4, 32, 512, 16, 512], P(None, 'row', None, 'col'), may hold values from -6 to 6
Outputs:
- diagonal_factor: float32 [16, 32, 32, 16], P(None, 'row', None, 'col')
- panel_factor: bfloat16 [4, 32, 512, 512], P(None, 'row', 'col')
- updated_trailing: bfloat16 [4, 32, 512, 16, 512], P(None, 'row', None, 'col')
The draws below stay inside these ranges and needn't reach their ends.
Inputs may be any that keep to these rules, and one draw needn't show every extreme that they name: `diagonal_tile`: symmetric positive definite: a Matern covariance of sites a few kilometres apart plus a nugget.
All inputs are finite; a program needn't handle non-finite values.
Results may differ from the reference program's by a relative error of at most 0.0053.
Values may be sent and summed in bfloat16 or wider, within the bound.
No kernel may reach another device: no remote copies, remote signals or barrier semaphores. Data moves between devices by JAX's collectives and lax.ppermute only.
A program may use at most 64 MiB of HBM per device.

```python
import jax
import jax.numpy as jnp
from jax import lax

NB = 512
RT = 4
NCOLS = 16
N_ROW = 32
N_COL = 16


def matern_tile(jitter, scales, reach, nugget):
    index = jnp.arange(NB)
    across = (index % 16).astype(jnp.float32) + jitter[0]
    down = (index // 16).astype(jnp.float32) + jitter[1]
    east = across[:, None] - across[None, :]
    north = down[:, None] - down[None, :]
    distance = jnp.sqrt(east * east + north * north)
    scaled = distance * (3.0 ** 0.5 / reach)
    kernel = (1.0 + scaled) * jnp.exp(-scaled)
    identity = jnp.eye(NB, dtype=jnp.float32)
    return scales[:, None] * scales[None, :] * kernel + nugget * identity


def draw_diagonal_tile(key, part):
    key = jax.random.fold_in(key, 11)
    first, second = jax.random.split(key)
    jitter = jax.random.uniform(first, (2, NB), jnp.float32, -0.3, 0.3)
    scales = jax.random.uniform(second, (NB,), jnp.float32, 0.85, 1.2)
    return matern_tile(jitter, scales, 5.0, 0.5)


def steps_of(rng, dims, cuts, least, top_value):
    def one(axis_at, parts):
        steps = jax.random.uniform(jax.random.fold_in(jax.random.fold_in(rng, 6), axis_at), (parts,), jnp.float32, least / len(cuts), top_value / len(cuts))
        return jnp.repeat(jnp.exp(steps), dims[axis_at] // parts).reshape((-1,) + (1,) * (len(dims) - axis_at - 1))

    gain = one(*cuts[0])
    for cut in cuts[1:]:
        gain = gain * one(*cut)
    return gain


def noise(stream_key, extent, spread, bound, shards=(), held_as=jnp.bfloat16):
    drawn = jax.random.normal(stream_key, extent, jnp.float32) * spread
    if len(shards) > 0:
        drawn = steps_of(stream_key, extent, shards, -0.22, 0.18) * drawn
    return jnp.clip(drawn, min=-bound, max=bound).astype(held_as)


def setup_inputs(seed: int = 0) -> dict:
    key_list = jax.random.split(jax.random.key(seed), 4)
    return {
        "panel": noise(key_list[0], (RT, N_ROW, NB, NB), (NB ** -0.25), 1.25, ((1, 32), (2, 16))),
        "diagonal_tile": draw_diagonal_tile(jax.random.fold_in(key_list[3], 71), 0),
        "trailing": noise(key_list[2], (RT, N_ROW, NB, NCOLS, NB), 1.0, 6.0, ((1, 32), (3, 16))),
    }


def reference(panel, diagonal_tile, trailing):
    factor = jnp.linalg.cholesky(diagonal_tile)
    inverse = lax.linalg.triangular_solve(factor, jnp.eye(NB, dtype=jnp.float32), left_side=True, lower=True)
    flat = panel.reshape(-1, NB).astype(jnp.float32)
    solved = jnp.dot(flat, inverse.T, precision=lax.Precision.HIGHEST).astype(jnp.bfloat16).reshape(panel.shape)
    column = solved[0, :N_COL].astype(jnp.float32)

    def update(pair):
        rows, current = pair
        product = jnp.einsum('rap,cbp->racb', rows.astype(jnp.float32), column)
        return (current.astype(jnp.float32) - product).astype(jnp.bfloat16)
    updated = lax.map(update, (solved, trailing))
    cyclic = factor.reshape(NB // N_ROW, N_ROW, NB // N_COL, N_COL)
    return (cyclic, solved, updated)
```

```python
import jax
import jax.numpy as jnp
from jax import lax
from jax.experimental import pallas as pl
from jax.experimental.pallas import tpu as pltpu
from jax.sharding import PartitionSpec as P

NB = 512
BLOCK = 128
F32, BF16 = jnp.float32, jnp.bfloat16
NT = (((1,), (1,)), ((), ()))
NN = (((1,), (0,)), ((), ()))


def split(x):
    high = x.astype(BF16)
    return high, (x - high.astype(F32)).astype(BF16)


def dot(a, b, dims):
    return lax.dot_general(a, b, dims, preferred_element_type=F32)


def dot_split(a, b, dims):
    a_high, a_low = split(a)
    b_high, b_low = split(b)
    return dot(a_high, b_high, dims) + (dot(a_high, b_low, dims) + dot(a_low, b_high, dims))


def over_lanes(x, j):
    return jnp.broadcast_to(x[:, j : j + 1], x.shape)


def over_rows(x, k):
    return jnp.broadcast_to(x[k : k + 1, :], x.shape)


def factor_block(block):
    row = lax.broadcasted_iota(jnp.int32, (8, BLOCK), 0)
    lane = lax.broadcasted_iota(jnp.int32, (8, BLOCK), 1)
    count = BLOCK // 8
    left = [block[8 * i : 8 * i + 8, :] for i in range(count)]
    right = [jnp.where(lane == row + 8 * i, 1.0, 0.0).astype(F32) for i in range(count)]
    upper, inverse = [], []
    for b in range(count):
        cols = {i: [over_lanes(left[i], 8 * b + j) for j in range(8)] for i in range(b, count)}
        own = cols[b]
        pivots = jnp.ones((8, BLOCK), F32)
        for k in range(8):
            pivot = over_rows(own[k], k)
            recip = 1.0 / pivot
            pivots = jnp.where(row == k, pivot, pivots)
            entries = {j: over_rows(own[j], k) for j in range(k + 1, 8)}
            mult = jnp.where(row > k, own[k] * recip, 0.0)
            left_row, right_row = over_rows(left[b], k), over_rows(right[b], k)
            left[b] = left[b] - mult * left_row
            right[b] = right[b] - mult * right_row
            for j in range(k + 1, 8):
                own[j] = own[j] - mult * entries[j]
            for i in range(b + 1, count):
                below = cols[i]
                mult = below[k] * recip
                for j in range(k + 1, 8):
                    below[j] = below[j] - mult * entries[j]
                left[i] = left[i] - mult * left_row
                right[i] = right[i] - mult * right_row
        scale = lax.rsqrt(pivots)
        upper.append(jnp.where(lane >= row + 8 * b, left[b] * scale, 0.0))
        inverse.append(right[b] * scale)
    return jnp.concatenate(upper, 0), jnp.concatenate(inverse, 0)


def factor_kernel(at_ref, tile_ref, own_ref, high_ref, low_ref, work, factor, inverse):
    work[...] = tile_ref[...]
    factor[...] = jnp.zeros_like(factor)
    inverse[...] = jnp.zeros_like(inverse)
    for start in range(0, NB, BLOCK):
        here = pl.ds(start, BLOCK)
        before = pl.ds(0, start)
        upto = pl.ds(0, start + BLOCK)
        after = pl.ds(start + BLOCK, NB - start - BLOCK)
        upper, block_inverse = factor_block(work[here, here])
        factor[here, here] = upper.T
        inverse[here, here] = block_inverse
        if start:
            inverse[here, before] = dot_split(block_inverse, inverse[here, before], NN)
        if start + BLOCK < NB:
            below = dot_split(work[after, here], block_inverse, NT)
            factor[after, here] = below
            work[after, after] = work[after, after] - dot_split(below, below, NT)
            inverse[after, upto] = inverse[after, upto] - dot_split(below, inverse[here, upto], NN)
    high, low = split(inverse[...])
    high_ref[...] = high
    low_ref[...] = low
    count_a, count_b = own_ref.shape
    step = NB // count_a
    rows = jnp.concatenate([factor[pl.ds(a * step + at_ref[0], 1), :] for a in range(count_a)], 0)
    source = lax.broadcasted_iota(jnp.int32, (NB, BLOCK), 0)
    target = lax.broadcasted_iota(jnp.int32, (NB, BLOCK), 1)
    pick = jnp.where(source == target * (NB // count_b) + at_ref[1], 1.0, 0.0).astype(BF16)
    first, rest = split(rows)
    second, third = split(rows - first.astype(F32))
    picked = dot(first, pick, NN) + (dot(second, pick, NN) + dot(third, pick, NN))
    own_ref[...] = picked[:, :count_b]


def update_kernel(at_ref, high_ref, low_ref, column_ref, panel_ref, trailing_ref, own_ref, out_ref, column, solved):
    high, low = high_ref[...], low_ref[...]

    @pl.when(pl.program_id(0) == 0)
    def _():
        tile = column_ref[...].astype(BF16)
        column[...] = (dot(tile, high, NT) + dot(tile, low, NT)).astype(BF16)

    rows = panel_ref[...].reshape(NB, NB)
    result = (dot(rows, high, NT) + dot(rows, low, NT)).astype(BF16)
    solved[...] = result
    strip = own_ref.shape[1]
    own_ref[0] = solved[pl.ds(pl.multiple_of(at_ref[1] * strip, strip), strip), :]
    product = dot(result, column[...], NT)
    out_ref[0] = (trailing_ref[0].astype(F32) - product).astype(BF16)


def to_all(x, axis):
    count = lax.axis_size(axis)
    return lax.all_to_all(jnp.broadcast_to(x[None], (count,) + x.shape), axis, 0, 0)


def on_device(panel, diagonal_tile, trailing):
    rows_count = lax.axis_size("row")
    cols_count = lax.axis_size("col")
    tiles = panel.shape[0]
    strip = panel.shape[2]
    half = NB // rows_count
    at = jnp.stack([lax.axis_index("row"), lax.axis_index("col")]).astype(jnp.int32)
    panel = panel.reshape(tiles, strip, NB)
    trailing = trailing.reshape(tiles, NB, NB)

    gathered = lax.all_gather(panel, "col")

    piece = jnp.zeros((half, NB), F32)
    for h in range(2):
        pairs = [
            (c * cols_count + s, (2 * s + h) * cols_count + c)
            for c in range(cols_count)
            for s in range(cols_count)
        ]
        piece = piece + lax.ppermute(panel[0, h * half : (h + 1) * half], ("row", "col"), pairs).astype(F32)

    pieces = to_all(diagonal_tile, "col")
    band = pieces.transpose(1, 0, 2).reshape(-1, NB)
    tile = to_all(band, "row").reshape(NB, NB)
    column = to_all(piece, "row").reshape(NB, NB)

    params = pltpu.CompilerParams(vmem_limit_bytes=48 << 20)
    smem = pl.BlockSpec(memory_space=pltpu.SMEM)
    own_factor, high, low = pl.pallas_call(
        factor_kernel,
        in_specs=[smem, pl.BlockSpec(memory_space=pltpu.VMEM)],
        out_shape=[
            jax.ShapeDtypeStruct((NB // rows_count, NB // cols_count), F32),
            jax.ShapeDtypeStruct((NB, NB), BF16),
            jax.ShapeDtypeStruct((NB, NB), BF16),
        ],
        scratch_shapes=[pltpu.VMEM((NB, NB), F32)] * 3,
        compiler_params=params,
        cost_estimate=pl.CostEstimate(flops=12 * NB**3, bytes_accessed=3 << 20, transcendentals=0),
    )(at, tile)

    whole = pl.BlockSpec((NB, NB), lambda t: (0, 0))
    own_strips, updated = pl.pallas_call(
        update_kernel,
        grid=(tiles,),
        in_specs=[
            smem,
            whole,
            whole,
            whole,
            pl.BlockSpec((cols_count, 1, strip, NB), lambda t: (0, t, 0, 0)),
            pl.BlockSpec((1, NB, NB), lambda t: (t, 0, 0)),
        ],
        out_specs=[
            pl.BlockSpec((1, strip, NB), lambda t: (t, 0, 0)),
            pl.BlockSpec((1, NB, NB), lambda t: (t, 0, 0)),
        ],
        out_shape=[
            jax.ShapeDtypeStruct((tiles, strip, NB), BF16),
            jax.ShapeDtypeStruct((tiles, NB, NB), BF16),
        ],
        scratch_shapes=[pltpu.VMEM((NB, NB), BF16)] * 2,
        compiler_params=params,
        cost_estimate=pl.CostEstimate(flops=30 * NB**3, bytes_accessed=8 << 20, transcendentals=0),
    )(at, high, low, column, gathered, trailing)

    return (
        own_factor.reshape(NB // rows_count, 1, NB // cols_count, 1),
        own_strips.reshape(tiles, 1, strip, NB),
        updated.reshape(tiles, 1, NB, 1, NB),
    )


def solution(mesh):
    in_specs = (P(None, "row", "col", None), P("row", "col"), P(None, "row", None, "col", None))
    out_specs = (
        P(None, "row", None, "col"),
        P(None, "row", "col", None),
        P(None, "row", None, "col", None),
    )
    return jax.shard_map(
        on_device, mesh=mesh, in_specs=in_specs, out_specs=out_specs, check_vma=False
    )
```

```python
import jax
import jax.numpy as jnp
from jax import lax
from jax.experimental import pallas as pl
from jax.experimental.pallas import tpu as pltpu
from jax.sharding import PartitionSpec as P

NB = 512
BLOCK = 128
LANES = 128
F32, BF16 = jnp.float32, jnp.bfloat16
NT = (((1,), (1,)), ((), ()))
NN = (((1,), (0,)), ((), ()))


def split(x):
    high = x.astype(BF16)
    return high, (x - high.astype(F32)).astype(BF16)


def dot(a, b, dims):
    return lax.dot_general(a, b, dims, preferred_element_type=F32)


def dot_split(a, b, dims):
    a_high, a_low = split(a)
    b_high, b_low = split(b)
    return dot(a_high, b_high, dims) + (dot(a_high, b_low, dims) + dot(a_low, b_high, dims))


def over_lanes(x, j):
    return jnp.broadcast_to(x[:, j : j + 1], x.shape)


def over_rows(x, k):
    return jnp.broadcast_to(x[k : k + 1, :], x.shape)


def total(terms):
    while len(terms) > 1:
        terms = [sum(terms[i : i + 2]) for i in range(0, len(terms), 2)]
    return terms[0]


def factor_block(block):
    row = lax.broadcasted_iota(jnp.int32, (8, BLOCK), 0)
    lane = lax.broadcasted_iota(jnp.int32, (8, BLOCK), 1)
    count = BLOCK // 8
    work = [block[8 * i : 8 * i + 8, :] for i in range(count)]
    upper, inverse = [], []

    def spread_columns(i, b):
        return [over_lanes(work[i], 8 * b + j) for j in range(8)]

    def eliminate(i, b, weights, columns):
        inside = (lane >= 8 * b) & (lane < 8 * b + 8)
        terms = [columns[k] * weights[k] for k in range(8)]
        work[i] = jnp.where(inside, 0.0, work[i]) - total(terms)

    weights = None
    for b in range(count):
        inside = (lane >= 8 * b) & (lane < 8 * b + 8)
        own = spread_columns(b, b)
        if b:
            for i in range(b + 1, count):
                eliminate(i, b - 1, weights, spread_columns(i, b - 1))
        if b + 1 < count:
            following = spread_columns(b + 1, b)
        identity = jnp.where(lane == row + 8 * b, 1.0, 0.0).astype(F32)
        left = work[b]
        right = rows = jnp.where(inside, identity, work[b])
        scale = jnp.zeros((8, BLOCK), F32)
        cross = jnp.zeros((8, BLOCK), F32)
        for k in range(0, 8, 2):
            first, second = row == k, row == k + 1
            pair = first | second
            head, off, tail = over_rows(own[k], k), over_rows(own[k + 1], k), over_rows(own[k + 1], k + 1)
            det = head * tail - off * off
            recip = 1.0 / det
            lead = own[k] * tail - own[k + 1] * off
            trail = own[k + 1] * head - own[k] * off
            lead_all = jnp.where(first, -tail, jnp.where(second, off, lead))
            trail_all = jnp.where(first, off, jnp.where(second, -head, trail))
            for j in range(8):
                if j not in (k, k + 1):
                    change = lead_all * over_rows(own[j], k) + trail_all * over_rows(own[j], k + 1)
                    own[j] = jnp.where(pair, 0.0, own[j]) - recip * change
            own[k], own[k + 1] = -(recip * lead_all), -(recip * trail_all)
            if k < 6:
                lead = jnp.where(row > k + 1, lead, 0.0)
                trail = jnp.where(row > k + 1, trail, 0.0)
                left = left - recip * (lead * over_rows(left, k) + trail * over_rows(left, k + 1))
                right = right - recip * (lead * over_rows(right, k) + trail * over_rows(right, k + 1))
            root, root_det = lax.rsqrt(head), lax.rsqrt(det)
            scale = jnp.where(first, root, jnp.where(second, root_det * (head * root), scale))
            cross = jnp.where(second, -(off * root * root_det), cross)
        solved = total([own[j] * over_rows(rows, j) for j in range(8)])
        weights = [over_rows(solved, k) for k in range(8)]
        if b + 1 < count:
            eliminate(b + 1, b, weights, following)
        left = left * scale + pltpu.roll(left, 1, 0) * cross
        right = right * scale + pltpu.roll(right, 1, 0) * cross
        upper.append(jnp.where(lane >= row + 8 * b, left, 0.0))
        inverse.append(jnp.where(lane < 8 * b + 8, right, 0.0))
    return jnp.concatenate(upper, 0), jnp.concatenate(inverse, 0)


def solve(rows, high, low):
    return (dot(rows, high, NT) + dot(rows, low, NT)).astype(BF16)


def fold_kernel(at_ref, band_ref, out_ref):
    half = out_ref.shape[1]
    turned = pltpu.roll(band_ref[...], lax.rem(NB - at_ref[0] * half, NB), 1)
    high, low = split(turned)
    window = NB // 2
    lane = lax.broadcasted_iota(jnp.int32, (half, LANES), 1)
    high_end = high[:, window : window + LANES].astype(F32)
    low_end = pltpu.roll(low[:, window : window + LANES].astype(F32), half, 1)
    end = jnp.where(lane < half, high_end, jnp.where(lane < 2 * half, low_end, 0.0)).astype(BF16)
    block = jnp.concatenate([high[:, :window], low[:, :window], end], 1)
    for i in range(out_ref.shape[0]):
        out_ref[i] = block


def unfold(spread_ref, work, folded):
    count, half, _ = spread_ref.shape
    window = NB // 2
    lane = lax.broadcasted_iota(jnp.int32, (half, LANES), 1)
    for r in range(count):
        part = spread_ref[r].astype(F32)
        end = part[:, NB:]
        end = jnp.where(lane < half, end + pltpu.roll(end, LANES - half, 1), 0.0)
        line = jnp.concatenate([part[:, :window] + part[:, window:NB], end, jnp.zeros_like(end)], 1)
        folded[half * r : half * (r + 1), :] = pltpu.roll(line, half * r, 1) if r else line
    per_block = BLOCK // half
    row = lax.broadcasted_iota(jnp.int32, (BLOCK, BLOCK), 0) // half
    col = lax.broadcasted_iota(jnp.int32, (BLOCK, BLOCK), 1) // half
    for i in range(NB // BLOCK):
        for j in range(i + 1):
            here, there = pl.ds(BLOCK * i, BLOCK), pl.ds(BLOCK * j, BLOCK)
            gap = (i - j) * per_block
            if gap - per_block + 1 >= count // 2:
                work[here, there] = folded[here, there]
                continue
            block = folded[there, here].T
            if i == j:
                block = jnp.where(col >= row, folded[here, there], block)
            elif gap + per_block - 1 >= count // 2:
                block = jnp.where(row - col + gap >= count // 2, folded[here, there], block)
            work[here, there] = block


def factor_kernel(at_ref, spread_ref, own_ref, high_ref, low_ref, work, factor, inverse):
    unfold(spread_ref, work, factor)
    factor[...] = jnp.zeros_like(factor)
    inverse[...] = jnp.zeros_like(inverse)
    for start in range(0, NB, BLOCK):
        here = pl.ds(start, BLOCK)
        before = pl.ds(0, start)
        upto = pl.ds(0, start + BLOCK)
        after = pl.ds(start + BLOCK, NB - start - BLOCK)
        upper, block_inverse = factor_block(work[here, here])
        factor[here, here] = upper.T
        inverse[here, here] = block_inverse
        if start:
            inverse[here, before] = dot_split(block_inverse, inverse[here, before], NN)
        if start + BLOCK < NB:
            below = dot_split(work[after, here], block_inverse, NT)
            factor[after, here] = below
            work[after, after] = work[after, after] - dot_split(below, below, NT)
            inverse[after, upto] = inverse[after, upto] - dot_split(below, inverse[here, upto], NN)
    high, low = split(inverse[...])
    high_ref[...] = high
    low_ref[...] = low
    count_a, count_b = own_ref.shape
    step = NB // count_a
    rows = jnp.concatenate([factor[pl.ds(a * step + at_ref[0], 1), :] for a in range(count_a)], 0)
    source = lax.broadcasted_iota(jnp.int32, (NB, BLOCK), 0)
    target = lax.broadcasted_iota(jnp.int32, (NB, BLOCK), 1)
    pick = jnp.where(source == target * (NB // count_b) + at_ref[1], 1.0, 0.0).astype(BF16)
    first, rest = split(rows)
    second, third = split(rows - first.astype(F32))
    picked = dot(first, pick, NN) + (dot(second, pick, NN) + dot(third, pick, NN))
    own_ref[...] = picked[:, :count_b]


def update_kernel(at_ref, high_ref, low_ref, tile_ref, panel_ref, trailing_ref, own_ref, out_ref, column, solved):
    high, low = high_ref[...], low_ref[...]

    strip = own_ref.shape[1]

    @pl.when(pl.program_id(0) == 0)
    def _():
        column[...] = solve(tile_ref[: NB // strip].reshape(NB, NB), high, low)

    rows = solve(panel_ref[...].reshape(NB, NB), high, low)
    solved[...] = rows
    own_ref[0] = solved[pl.ds(pl.multiple_of(at_ref[1] * strip, strip), strip), :]
    out_ref[0] = (trailing_ref[0].astype(F32) - dot(rows, column[...], NT)).astype(BF16)


def on_device(panel, diagonal_tile, trailing):
    rows_count = lax.axis_size("row")
    cols_count = lax.axis_size("col")
    tiles = panel.shape[0]
    strip = panel.shape[2]
    half = NB // rows_count
    at = jnp.stack([lax.axis_index("row"), lax.axis_index("col")]).astype(jnp.int32)
    panel = panel.reshape(tiles, strip, NB)
    trailing = trailing.reshape(tiles, NB, NB)

    gathered = lax.all_gather(panel, "col")

    pairs = [(c * cols_count + s, s * cols_count + c) for c in range(cols_count) for s in range(cols_count)]
    piece = lax.ppermute(panel[0], ("row", "col"), pairs)

    piece_rows, piece_cols = diagonal_tile.shape
    own = diagonal_tile.reshape(-1, LANES)
    pieces = lax.all_to_all(jnp.broadcast_to(own[None], (cols_count,) + own.shape), "col", 0, 0)
    band = pieces.reshape(cols_count, piece_rows, piece_cols).transpose(1, 0, 2).reshape(-1, NB)
    vmem = pl.BlockSpec(memory_space=pltpu.VMEM)
    smem = pl.BlockSpec(memory_space=pltpu.SMEM)
    folded = pl.pallas_call(
        fold_kernel,
        in_specs=[smem, vmem],
        out_specs=vmem,
        out_shape=jax.ShapeDtypeStruct((rows_count, half, NB + LANES), BF16),
    )(at, band)
    spread = lax.all_to_all(folded, "row", 0, 0)
    piece = lax.optimization_barrier((piece, spread))[0]
    tile = lax.all_to_all(jnp.broadcast_to(piece[None], (rows_count,) + piece.shape), "row", 0, 0)

    params = pltpu.CompilerParams(vmem_limit_bytes=32 << 20)
    own_factor, high, low = pl.pallas_call(
        factor_kernel,
        grid=(1,),
        in_specs=[smem, pl.BlockSpec(spread.shape, lambda i: (0, 0, 0))],
        out_specs=[pl.BlockSpec((NB // rows_count, NB // cols_count), lambda i: (0, 0))]
        + [pl.BlockSpec((NB, NB), lambda i: (0, 0))] * 2,
        out_shape=[
            jax.ShapeDtypeStruct((NB // rows_count, NB // cols_count), F32),
        ]
        + [jax.ShapeDtypeStruct((NB, NB), BF16)] * 2,
        scratch_shapes=[pltpu.VMEM((NB, NB), F32)] * 3,
        compiler_params=params,
        cost_estimate=pl.CostEstimate(flops=12 * NB**3, bytes_accessed=3 << 20, transcendentals=0),
    )(at, spread)

    gathered = pltpu.with_memory_space_constraint(gathered, pltpu.HBM)
    trailing = pltpu.with_memory_space_constraint(trailing, pltpu.HBM)
    own_strips, updated = pl.pallas_call(
        update_kernel,
        grid=(tiles,),
        in_specs=[
            smem,
            vmem,
            vmem,
            vmem,
            pl.BlockSpec((cols_count, 1, strip, NB), lambda t: (0, t, 0, 0)),
            pl.BlockSpec((1, NB, NB), lambda t: (t, 0, 0)),
        ],
        out_specs=[
            pl.BlockSpec((1, strip, NB), lambda t: (t, 0, 0)),
            pl.BlockSpec((1, NB, NB), lambda t: (t, 0, 0)),
        ],
        out_shape=[
            jax.ShapeDtypeStruct((tiles, strip, NB), BF16),
            jax.ShapeDtypeStruct((tiles, NB, NB), BF16),
        ],
        scratch_shapes=[pltpu.VMEM((NB, NB), BF16)] * 2,
        compiler_params=params,
        cost_estimate=pl.CostEstimate(flops=30 * NB**3, bytes_accessed=8 << 20, transcendentals=0),
    )(at, high, low, tile, gathered, trailing)

    return (
        own_factor.reshape(NB // rows_count, 1, NB // cols_count, 1),
        own_strips.reshape(tiles, 1, strip, NB),
        updated.reshape(tiles, 1, NB, 1, NB),
    )


def solution(mesh):
    in_specs = (P(None, "row", "col", None), P("row", "col"), P(None, "row", None, "col", None))
    out_specs = (
        P(None, "row", None, "col"),
        P(None, "row", "col", None),
        P(None, "row", None, "col", None),
    )
    return jax.shard_map(
        on_device, mesh=mesh, in_specs=in_specs, out_specs=out_specs, check_vma=False
    )
```

```python
import jax
import jax.numpy as jnp
from jax import lax
from jax.experimental import pallas as pl
from jax.experimental.pallas import tpu as pltpu
from jax.sharding import PartitionSpec as P

NB = 512
BLOCK = 128
LANES = 128
FIRST = 1
F32, BF16 = jnp.float32, jnp.bfloat16
NT = (((1,), (1,)), ((), ()))
NN = (((1,), (0,)), ((), ()))


def split(x):
    high = x.astype(BF16)
    return high, (x - high.astype(F32)).astype(BF16)


def dot(a, b, dims):
    return lax.dot_general(a, b, dims, preferred_element_type=F32)


def dot_split(a, b, dims):
    a_high, a_low = split(a)
    b_high, b_low = split(b)
    return dot(a_high, b_high, dims) + (dot(a_high, b_low, dims) + dot(a_low, b_high, dims))


def over_lanes(x, j):
    return jnp.broadcast_to(x[:, j : j + 1], x.shape)


def over_rows(x, k):
    return jnp.broadcast_to(x[k : k + 1, :], x.shape)


def total(terms):
    while len(terms) > 1:
        terms = [sum(terms[i : i + 2]) for i in range(0, len(terms), 2)]
    return terms[0]


def factor_block(block):
    row = lax.broadcasted_iota(jnp.int32, (8, BLOCK), 0)
    lane = lax.broadcasted_iota(jnp.int32, (8, BLOCK), 1)
    count = BLOCK // 8
    work = [block[8 * i : 8 * i + 8, :] for i in range(count)]
    upper, inverse = [], []

    def spread_columns(i, b):
        return [over_lanes(work[i], 8 * b + j) for j in range(8)]

    def eliminate(i, b, weights, columns):
        inside = (lane >= 8 * b) & (lane < 8 * b + 8)
        terms = [columns[k] * weights[k] for k in range(8)]
        work[i] = jnp.where(inside, 0.0, work[i]) - total(terms)

    weights = None
    for b in range(count):
        inside = (lane >= 8 * b) & (lane < 8 * b + 8)
        own = spread_columns(b, b)
        if b:
            for i in range(b + 1, count):
                eliminate(i, b - 1, weights, spread_columns(i, b - 1))
        if b + 1 < count:
            following = spread_columns(b + 1, b)
        identity = jnp.where(lane == row + 8 * b, 1.0, 0.0).astype(F32)
        left = work[b]
        right = rows = jnp.where(inside, identity, work[b])
        scale = jnp.zeros((8, BLOCK), F32)
        cross = jnp.zeros((8, BLOCK), F32)
        for k in range(0, 8, 2):
            first, second = row == k, row == k + 1
            pair = first | second
            head, off, tail = over_rows(own[k], k), over_rows(own[k + 1], k), over_rows(own[k + 1], k + 1)
            det = head * tail - off * off
            recip = 1.0 / det
            lead = own[k] * tail - own[k + 1] * off
            trail = own[k + 1] * head - own[k] * off
            lead_all = jnp.where(first, -tail, jnp.where(second, off, lead))
            trail_all = jnp.where(first, off, jnp.where(second, -head, trail))
            for j in range(8):
                if j not in (k, k + 1):
                    change = lead_all * over_rows(own[j], k) + trail_all * over_rows(own[j], k + 1)
                    own[j] = jnp.where(pair, 0.0, own[j]) - recip * change
            own[k], own[k + 1] = -(recip * lead_all), -(recip * trail_all)
            if k < 6:
                lead = jnp.where(row > k + 1, lead, 0.0)
                trail = jnp.where(row > k + 1, trail, 0.0)
                left = left - recip * (lead * over_rows(left, k) + trail * over_rows(left, k + 1))
                right = right - recip * (lead * over_rows(right, k) + trail * over_rows(right, k + 1))
            root, root_det = lax.rsqrt(head), lax.rsqrt(det)
            scale = jnp.where(first, root, jnp.where(second, root_det * (head * root), scale))
            cross = jnp.where(second, -(off * root * root_det), cross)
        solved = total([own[j] * over_rows(rows, j) for j in range(8)])
        weights = [over_rows(solved, k) for k in range(8)]
        if b + 1 < count:
            eliminate(b + 1, b, weights, following)
        left = left * scale + pltpu.roll(left, 1, 0) * cross
        right = right * scale + pltpu.roll(right, 1, 0) * cross
        upper.append(jnp.where(lane >= row + 8 * b, left, 0.0))
        inverse.append(jnp.where(lane < 8 * b + 8, right, 0.0))
    return jnp.concatenate(upper, 0), jnp.concatenate(inverse, 0)


def solve(rows, high, low):
    return (dot(rows, high, NT) + dot(rows, low, NT)).astype(BF16)


def fold_kernel(at_ref, band_ref, out_ref):
    half = out_ref.shape[1]
    turned = pltpu.roll(band_ref[...], lax.rem(NB - at_ref[0] * half, NB), 1)
    high, low = split(turned)
    window = NB // 2
    lane = lax.broadcasted_iota(jnp.int32, (half, LANES), 1)
    high_end = high[:, window : window + LANES].astype(F32)
    low_end = pltpu.roll(low[:, window : window + LANES].astype(F32), half, 1)
    end = jnp.where(lane < half, high_end, jnp.where(lane < 2 * half, low_end, 0.0)).astype(BF16)
    block = jnp.concatenate([high[:, :window], low[:, :window], end], 1)
    for i in range(out_ref.shape[0]):
        out_ref[i] = block


def unfold(spread_ref, folded):
    count, half, _ = spread_ref.shape
    window = NB // 2
    lane = lax.broadcasted_iota(jnp.int32, (half, LANES), 1)
    for r in range(count):
        part = spread_ref[r, :, : NB + LANES].astype(F32)
        end = part[:, NB:]
        end = jnp.where(lane < half, end + pltpu.roll(end, LANES - half, 1), 0.0)
        line = jnp.concatenate([part[:, :window] + part[:, window:NB], end, jnp.zeros_like(end)], 1)
        folded[half * r : half * (r + 1), :] = pltpu.roll(line, half * r, 1) if r else line


def folded_block(folded, i, j, half):
    count, per_block = NB // half, BLOCK // half
    row = lax.broadcasted_iota(jnp.int32, (BLOCK, BLOCK), 0) // half
    col = lax.broadcasted_iota(jnp.int32, (BLOCK, BLOCK), 1) // half
    here, there = pl.ds(BLOCK * i, BLOCK), pl.ds(BLOCK * j, BLOCK)
    gap = (i - j) * per_block
    if gap - per_block + 1 >= count // 2:
        return folded[here, there]
    block = folded[there, here].T
    if i == j:
        return jnp.where(col >= row, folded[here, there], block)
    if gap + per_block - 1 >= count // 2:
        return jnp.where(row - col + gap >= count // 2, folded[here, there], block)
    return block


def factor_steps(steps, work, pending, factor, inverse):
    blocks = NB // BLOCK
    for p in steps:
        here = pl.ds(BLOCK * p, BLOCK)
        upper, block_inverse = factor_block(work[p, p])
        below = {}
        for q in range(p + 1, blocks):
            below[q] = dot_split(work[q, p], block_inverse, NT)
            for r in range(p + 1, q + 1):
                work[q, r] = work[q, r] - dot_split(below[q], below[r], NT)
        factor[here, here] = upper.T
        rows = {r: dot_split(block_inverse, pending[p, r], NN) for r in range(p)}
        rows[p] = block_inverse
        for r in range(p + 1):
            inverse[here, pl.ds(BLOCK * r, BLOCK)] = rows[r]
        for q in range(p + 1, blocks):
            factor[pl.ds(BLOCK * q, BLOCK), here] = below[q]
            for r in range(p + 1):
                change = dot_split(below[q], rows[r], NN)
                pending[q, r] = pending[q, r] - change if r < p else -change


def block_at(i, j):
    return pl.ds(BLOCK * i, BLOCK), pl.ds(BLOCK * j, BLOCK)


def first_kernel(spread_ref, factor, state, folded):
    unfold(spread_ref, folded)
    factor[...] = jnp.zeros_like(factor)
    state[...] = jnp.zeros_like(state)
    blocks = NB // BLOCK
    half = spread_ref.shape[1]
    work = {(i, j): folded_block(folded, i, j, half) for j in range(blocks) for i in range(j, blocks)}
    pending = {}
    factor_steps(range(FIRST), work, pending, factor, state)
    for q in range(FIRST, blocks):
        for r in range(q + 1):
            state[block_at(q, r)] = pending[q, r] if r < FIRST else work[q, r]


def second_kernel(at_ref, factor_ref, state_ref, own_ref, high_ref, low_ref, factor, inverse):
    factor[...] = factor_ref[...]
    inverse[...] = state_ref[...]
    blocks = NB // BLOCK
    todo = range(FIRST, blocks)
    pending = {(q, r): state_ref[block_at(q, r)] for q in todo for r in range(FIRST)}
    work = {(q, r): state_ref[block_at(q, r)] for r in todo for q in range(r, blocks)}
    factor_steps(todo, work, pending, factor, inverse)
    high, low = split(inverse[...])
    high_ref[...] = high
    low_ref[...] = low
    count_a, count_b = own_ref.shape
    step = NB // count_a
    rows = jnp.concatenate([factor[pl.ds(a * step + at_ref[0], 1), :] for a in range(count_a)], 0)
    source = lax.broadcasted_iota(jnp.int32, (NB, BLOCK), 0)
    target = lax.broadcasted_iota(jnp.int32, (NB, BLOCK), 1)
    pick = jnp.where(source == target * (NB // count_b) + at_ref[1], 1.0, 0.0).astype(BF16)
    first, rest = split(rows)
    second, third = split(rows - first.astype(F32))
    picked = dot(first, pick, NN) + (dot(second, pick, NN) + dot(third, pick, NN))
    own_ref[...] = picked[:, :count_b]


def prepare_kernel(high_ref, low_ref, tile_ref, panel_ref, own_ref, out_high_ref, out_low_ref):
    high, low = high_ref[...], low_ref[...]
    tiles, strip, _ = panel_ref.shape
    column = solve(tile_ref[: NB // strip].reshape(NB, NB), high, low)
    own_ref[...] = solve(panel_ref[...].reshape(tiles * strip, NB), high, low).reshape(tiles, strip, NB)
    out_high_ref[...], out_low_ref[...] = split(dot(column, high, NN) + dot(column, low, NN))


def update_kernel(high_ref, low_ref, panel_ref, trailing_ref, out_ref):
    rows = panel_ref[...].reshape(NB, NB)
    product = dot(rows, high_ref[...], NT) + dot(rows, low_ref[...], NT)
    out_ref[0] = (trailing_ref[0].astype(F32) - product).astype(BF16)


def whole(x):
    return pl.BlockSpec(x.shape, lambda i: (0,) * x.ndim)


def on_device(panel, diagonal_tile, trailing):
    rows_count = lax.axis_size("row")
    cols_count = lax.axis_size("col")
    tiles = panel.shape[0]
    strip = panel.shape[2]
    half = NB // rows_count
    at = jnp.stack([lax.axis_index("row"), lax.axis_index("col")]).astype(jnp.int32)
    panel = panel.reshape(tiles, strip, NB)
    trailing = trailing.reshape(tiles, NB, NB)

    gathered = lax.all_gather(panel, "col")

    pairs = [(c * cols_count + s, s * cols_count + c) for c in range(cols_count) for s in range(cols_count)]
    piece = lax.ppermute(panel[0], ("row", "col"), pairs)

    piece_rows, piece_cols = diagonal_tile.shape
    own = diagonal_tile.reshape(-1, LANES)
    pieces = lax.all_to_all(jnp.broadcast_to(own[None], (cols_count,) + own.shape), "col", 0, 0)
    band = pieces.reshape(cols_count, piece_rows, piece_cols).transpose(1, 0, 2).reshape(-1, NB)
    vmem = pl.BlockSpec(memory_space=pltpu.VMEM)
    smem = pl.BlockSpec(memory_space=pltpu.SMEM)
    folded = pl.pallas_call(
        fold_kernel,
        in_specs=[smem, vmem],
        out_specs=vmem,
        out_shape=jax.ShapeDtypeStruct((rows_count, half, NB + LANES), BF16),
    )(at, band)
    spread = lax.all_to_all(folded, "row", 0, 0)
    params = pltpu.CompilerParams(vmem_limit_bytes=16 << 20)
    full = jax.ShapeDtypeStruct((NB, NB), F32)
    half_tile = jax.ShapeDtypeStruct((NB, NB), BF16)
    cost = pl.CostEstimate(flops=6 * NB**3, bytes_accessed=3 << 20, transcendentals=0)
    factor, state = pl.pallas_call(
        first_kernel,
        in_specs=[vmem],
        out_specs=[vmem] * 2,
        out_shape=[full] * 2,
        scratch_shapes=[pltpu.VMEM((NB, NB), F32)],
        compiler_params=params,
        cost_estimate=cost,
    )(spread)
    piece, factor, state = lax.optimization_barrier((piece, factor, state))
    tile = lax.all_to_all(jnp.broadcast_to(piece[None], (rows_count,) + piece.shape), "row", 0, 0)
    own_factor, high, low = pl.pallas_call(
        second_kernel,
        grid=(1,),
        in_specs=[smem, vmem, vmem],
        out_specs=[pl.BlockSpec((NB // rows_count, NB // cols_count), lambda i: (0, 0))]
        + [pl.BlockSpec((NB, NB), lambda i: (0, 0))] * 2,
        out_shape=[
            jax.ShapeDtypeStruct((NB // rows_count, NB // cols_count), F32),
            half_tile,
            half_tile,
        ],
        scratch_shapes=[pltpu.VMEM((NB, NB), F32)] * 2,
        compiler_params=params,
        cost_estimate=cost,
    )(at, factor, state)

    own_strips, high, low = pl.pallas_call(
        prepare_kernel,
        grid=(1,),
        in_specs=[whole(high), whole(low), whole(tile), whole(panel)],
        out_specs=[whole(panel), whole(high), whole(low)],
        out_shape=[jax.ShapeDtypeStruct((tiles, strip, NB), BF16), half_tile, half_tile],
        compiler_params=params,
        cost_estimate=pl.CostEstimate(flops=10 * NB**3, bytes_accessed=3 << 20, transcendentals=0),
    )(high, low, tile, panel)
    gathered = pltpu.with_memory_space_constraint(gathered, pltpu.HBM)
    trailing = pltpu.with_memory_space_constraint(trailing, pltpu.HBM)
    updated = pl.pallas_call(
        update_kernel,
        grid=(tiles,),
        in_specs=[
            whole(high),
            whole(low),
            pl.BlockSpec((cols_count, 1, strip, NB), lambda t: (0, t, 0, 0)),
            pl.BlockSpec((1, NB, NB), lambda t: (t, 0, 0)),
        ],
        out_specs=pl.BlockSpec((1, NB, NB), lambda t: (t, 0, 0)),
        out_shape=jax.ShapeDtypeStruct((tiles, NB, NB), BF16),
        compiler_params=params,
        cost_estimate=pl.CostEstimate(flops=16 * NB**3, bytes_accessed=6 << 20, transcendentals=0),
    )(high, low, gathered, trailing)

    return (
        own_factor.reshape(NB // rows_count, 1, NB // cols_count, 1),
        own_strips.reshape(tiles, 1, strip, NB),
        updated.reshape(tiles, 1, NB, 1, NB),
    )


def solution(mesh):
    in_specs = (P(None, "row", "col", None), P("row", "col"), P(None, "row", None, "col", None))
    out_specs = (
        P(None, "row", None, "col"),
        P(None, "row", "col", None),
        P(None, "row", None, "col", None),
    )
    return jax.shard_map(
        on_device, mesh=mesh, in_specs=in_specs, out_specs=out_specs, check_vma=False
    )
```

```python
import jax
import jax.numpy as jnp
from jax import lax
from jax.experimental import pallas as pl
from jax.experimental.pallas import tpu as pltpu
from jax.sharding import PartitionSpec as P

NB = 512
BLOCK = 128
LANES = 128
FIRST = 1
F32, BF16 = jnp.float32, jnp.bfloat16
NT = (((1,), (1,)), ((), ()))
NN = (((1,), (0,)), ((), ()))


def split(x):
    high = x.astype(BF16)
    return high, (x - high.astype(F32)).astype(BF16)


def dot(a, b, dims):
    return lax.dot_general(a, b, dims, preferred_element_type=F32)


def dot_split(a, b, dims):
    a_high, a_low = split(a)
    b_high, b_low = split(b)
    return dot(a_high, b_high, dims) + (dot(a_high, b_low, dims) + dot(a_low, b_high, dims))


def over_lanes(x, j):
    return jnp.broadcast_to(x[:, j : j + 1], x.shape)


def over_rows(x, k):
    return jnp.broadcast_to(x[k : k + 1, :], x.shape)


def total(terms):
    while len(terms) > 1:
        terms = [sum(terms[i : i + 2]) for i in range(0, len(terms), 2)]
    return terms[0]


def factor_block(block):
    row = lax.broadcasted_iota(jnp.int32, (8, BLOCK), 0)
    lane = lax.broadcasted_iota(jnp.int32, (8, BLOCK), 1)
    count = BLOCK // 8
    work = [block[8 * i : 8 * i + 8, :] for i in range(count)]
    upper, inverse = [], []

    def spread_columns(i, b):
        return [over_lanes(work[i], 8 * b + j) for j in range(8)]

    def eliminate(i, b, weights, columns):
        inside = (lane >= 8 * b) & (lane < 8 * b + 8)
        terms = [columns[k] * weights[k] for k in range(8)]
        work[i] = jnp.where(inside, 0.0, work[i]) - total(terms)

    weights = None
    for b in range(count):
        inside = (lane >= 8 * b) & (lane < 8 * b + 8)
        own = spread_columns(b, b)
        if b:
            for i in range(b + 1, count):
                eliminate(i, b - 1, weights, spread_columns(i, b - 1))
        if b + 1 < count:
            following = spread_columns(b + 1, b)
        identity = jnp.where(lane == row + 8 * b, 1.0, 0.0).astype(F32)
        left = work[b]
        right = rows = jnp.where(inside, identity, work[b])
        scale = jnp.zeros((8, BLOCK), F32)
        cross = jnp.zeros((8, BLOCK), F32)
        for k in range(0, 8, 2):
            first, second = row == k, row == k + 1
            pair = first | second
            head, off, tail = over_rows(own[k], k), over_rows(own[k + 1], k), over_rows(own[k + 1], k + 1)
            det = head * tail - off * off
            recip = 1.0 / det
            lead = own[k] * tail - own[k + 1] * off
            trail = own[k + 1] * head - own[k] * off
            lead_all = jnp.where(first, -tail, jnp.where(second, off, lead))
            trail_all = jnp.where(first, off, jnp.where(second, -head, trail))
            for j in range(8):
                if j not in (k, k + 1):
                    change = lead_all * over_rows(own[j], k) + trail_all * over_rows(own[j], k + 1)
                    own[j] = jnp.where(pair, 0.0, own[j]) - recip * change
            own[k], own[k + 1] = -(recip * lead_all), -(recip * trail_all)
            if k < 6:
                lead = jnp.where(row > k + 1, lead, 0.0)
                trail = jnp.where(row > k + 1, trail, 0.0)
                left = left - recip * (lead * over_rows(left, k) + trail * over_rows(left, k + 1))
                right = right - recip * (lead * over_rows(right, k) + trail * over_rows(right, k + 1))
            root, root_det = lax.rsqrt(head), lax.rsqrt(det)
            scale = jnp.where(first, root, jnp.where(second, root_det * (head * root), scale))
            cross = jnp.where(second, -(off * root * root_det), cross)
        solved = total([own[j] * over_rows(rows, j) for j in range(8)])
        weights = [over_rows(solved, k) for k in range(8)]
        if b + 1 < count:
            eliminate(b + 1, b, weights, following)
        left = left * scale + pltpu.roll(left, 1, 0) * cross
        right = right * scale + pltpu.roll(right, 1, 0) * cross
        upper.append(jnp.where(lane >= row + 8 * b, left, 0.0))
        inverse.append(jnp.where(lane < 8 * b + 8, right, 0.0))
    return jnp.concatenate(upper, 0), jnp.concatenate(inverse, 0)


def solve(rows, high, low):
    return (dot(rows, high, NT) + dot(rows, low, NT)).astype(BF16)


def fold_kernel(at_ref, band_ref, out_ref):
    half = out_ref.shape[1]
    turned = pltpu.roll(band_ref[...], lax.rem(NB - at_ref[0] * half, NB), 1)
    high, low = split(turned)
    window = NB // 2
    lane = lax.broadcasted_iota(jnp.int32, (half, LANES), 1)
    high_end = high[:, window : window + LANES].astype(F32)
    low_end = pltpu.roll(low[:, window : window + LANES].astype(F32), half, 1)
    end = jnp.where(lane < half, high_end, jnp.where(lane < 2 * half, low_end, 0.0)).astype(BF16)
    block = jnp.concatenate([high[:, :window], low[:, :window], end], 1)
    for i in range(out_ref.shape[0]):
        out_ref[i] = block


def unfold(spread_ref, folded):
    count, half, _ = spread_ref.shape
    window = NB // 2
    lane = lax.broadcasted_iota(jnp.int32, (half, LANES), 1)
    for r in range(count):
        part = spread_ref[r, :, : NB + LANES].astype(F32)
        end = part[:, NB:]
        end = jnp.where(lane < half, end + pltpu.roll(end, LANES - half, 1), 0.0)
        line = jnp.concatenate([part[:, :window] + part[:, window:NB], end, jnp.zeros_like(end)], 1)
        folded[half * r : half * (r + 1), :] = pltpu.roll(line, half * r, 1) if r else line


def folded_block(folded, i, j, half):
    count, per_block = NB // half, BLOCK // half
    row = lax.broadcasted_iota(jnp.int32, (BLOCK, BLOCK), 0) // half
    col = lax.broadcasted_iota(jnp.int32, (BLOCK, BLOCK), 1) // half
    here, there = pl.ds(BLOCK * i, BLOCK), pl.ds(BLOCK * j, BLOCK)
    gap = (i - j) * per_block
    if gap - per_block + 1 >= count // 2:
        return folded[here, there]
    block = folded[there, here].T
    if i == j:
        return jnp.where(col >= row, folded[here, there], block)
    if gap + per_block - 1 >= count // 2:
        return jnp.where(row - col + gap >= count // 2, folded[here, there], block)
    return block


def factor_steps(steps, work, pending, factor, inverse):
    blocks = NB // BLOCK
    for p in steps:
        here = pl.ds(BLOCK * p, BLOCK)
        upper, block_inverse = factor_block(work[p, p])
        below = {}
        for q in range(p + 1, blocks):
            below[q] = dot_split(work[q, p], block_inverse, NT)
            for r in range(p + 1, q + 1):
                work[q, r] = work[q, r] - dot_split(below[q], below[r], NT)
        factor[here, here] = upper.T
        rows = {r: dot_split(block_inverse, pending[p, r], NN) for r in range(p)}
        rows[p] = block_inverse
        for r in range(p + 1):
            inverse[here, pl.ds(BLOCK * r, BLOCK)] = rows[r]
        for q in range(p + 1, blocks):
            factor[pl.ds(BLOCK * q, BLOCK), here] = below[q]
            for r in range(p + 1):
                change = dot_split(below[q], rows[r], NN)
                pending[q, r] = pending[q, r] - change if r < p else -change


def block_at(i, j):
    return pl.ds(BLOCK * i, BLOCK), pl.ds(BLOCK * j, BLOCK)


def first_kernel(spread_ref, factor, state, folded):
    unfold(spread_ref, folded)
    factor[...] = jnp.zeros_like(factor)
    state[...] = jnp.zeros_like(state)
    blocks = NB // BLOCK
    half = spread_ref.shape[1]
    work = {(i, j): folded_block(folded, i, j, half) for j in range(blocks) for i in range(j, blocks)}
    pending = {}
    factor_steps(range(FIRST), work, pending, factor, state)
    for q in range(FIRST, blocks):
        for r in range(q + 1):
            state[block_at(q, r)] = pending[q, r] if r < FIRST else work[q, r]


def second_kernel(at_ref, factor_ref, state_ref, own_ref, high_ref, low_ref, factor, inverse):
    factor[...] = factor_ref[...]
    inverse[...] = state_ref[...]
    blocks = NB // BLOCK
    todo = range(FIRST, blocks)
    pending = {(q, r): state_ref[block_at(q, r)] for q in todo for r in range(FIRST)}
    work = {(q, r): state_ref[block_at(q, r)] for r in todo for q in range(r, blocks)}
    factor_steps(todo, work, pending, factor, inverse)
    high, low = split(inverse[...])
    high_ref[...] = high
    low_ref[...] = low
    count_a, count_b = own_ref.shape
    step = NB // count_a
    rows = jnp.concatenate([factor[pl.ds(a * step + at_ref[0], 1), :] for a in range(count_a)], 0)
    source = lax.broadcasted_iota(jnp.int32, (NB, BLOCK), 0)
    target = lax.broadcasted_iota(jnp.int32, (NB, BLOCK), 1)
    pick = jnp.where(source == target * (NB // count_b) + at_ref[1], 1.0, 0.0).astype(BF16)
    first, rest = split(rows)
    second, third = split(rows - first.astype(F32))
    picked = dot(first, pick, NN) + (dot(second, pick, NN) + dot(third, pick, NN))
    own_ref[...] = picked[:, :count_b]


def prepare_kernel(high_ref, low_ref, tile_ref, panel_ref, own_ref, out_high_ref, out_low_ref):
    high, low = high_ref[...], low_ref[...]
    tiles, strip, _ = panel_ref.shape
    column = solve(tile_ref[: NB // strip].reshape(NB, NB), high, low)
    own_ref[...] = solve(panel_ref[...].reshape(tiles * strip, NB), high, low).reshape(tiles, strip, NB)
    out_high_ref[...], out_low_ref[...] = split(dot(column, high, NN) + dot(column, low, NN))


def update_kernel(high_ref, low_ref, panel_ref, trailing_ref, out_ref):
    rows = panel_ref[...].reshape(NB, NB)
    product = dot(rows, high_ref[...], NT) + dot(rows, low_ref[...], NT)
    out_ref[0] = (trailing_ref[0].astype(F32) - product).astype(BF16)


def whole(x):
    return pl.BlockSpec(x.shape, lambda i: (0,) * x.ndim)


def on_device(panel, diagonal_tile, trailing):
    rows_count = lax.axis_size("row")
    cols_count = lax.axis_size("col")
    tiles = panel.shape[0]
    strip = panel.shape[2]
    half = NB // rows_count
    at = jnp.stack([lax.axis_index("row"), lax.axis_index("col")]).astype(jnp.int32)
    panel = panel.reshape(tiles, strip, NB)
    trailing = trailing.reshape(tiles, NB, NB)

    gathered = lax.all_gather(panel, "col")

    pairs = [(c * cols_count + s, s * cols_count + c) for c in range(cols_count) for s in range(cols_count)]
    piece = lax.ppermute(panel[0], ("row", "col"), pairs)

    piece_rows, piece_cols = diagonal_tile.shape
    own = diagonal_tile.reshape(-1, LANES)
    pieces = lax.all_to_all(jnp.broadcast_to(own[None], (cols_count,) + own.shape), "col", 0, 0)
    band = pieces.reshape(cols_count, piece_rows, piece_cols).transpose(1, 0, 2).reshape(-1, NB)
    vmem = pl.BlockSpec(memory_space=pltpu.VMEM)
    smem = pl.BlockSpec(memory_space=pltpu.SMEM)
    folded = pl.pallas_call(
        fold_kernel,
        in_specs=[smem, vmem],
        out_specs=vmem,
        out_shape=jax.ShapeDtypeStruct((rows_count, half, NB + LANES), BF16),
    )(at, band)
    spread = lax.all_to_all(folded, "row", 0, 0)
    params = pltpu.CompilerParams(vmem_limit_bytes=16 << 20)
    full = jax.ShapeDtypeStruct((NB, NB), F32)
    half_tile = jax.ShapeDtypeStruct((NB, NB), BF16)
    cost = pl.CostEstimate(flops=6 * NB**3, bytes_accessed=3 << 20, transcendentals=0)
    factor, state = pl.pallas_call(
        first_kernel,
        in_specs=[vmem],
        out_specs=[vmem] * 2,
        out_shape=[full] * 2,
        scratch_shapes=[pltpu.VMEM((NB, NB), F32)],
        compiler_params=params,
        cost_estimate=cost,
    )(spread)
    piece, factor, state = lax.optimization_barrier((piece, factor, state))
    tile = lax.all_to_all(jnp.broadcast_to(piece[None], (rows_count,) + piece.shape), "row", 0, 0)
    own_factor, high, low = pl.pallas_call(
        second_kernel,
        grid=(1,),
        in_specs=[smem, vmem, vmem],
        out_specs=[pl.BlockSpec((NB // rows_count, NB // cols_count), lambda i: (0, 0))]
        + [pl.BlockSpec((NB, NB), lambda i: (0, 0))] * 2,
        out_shape=[
            jax.ShapeDtypeStruct((NB // rows_count, NB // cols_count), F32),
            half_tile,
            half_tile,
        ],
        scratch_shapes=[pltpu.VMEM((NB, NB), F32)] * 2,
        compiler_params=params,
        cost_estimate=cost,
    )(at, factor, state)
    high, low = (pltpu.with_memory_space_constraint(x, pltpu.HBM) for x in (high, low))

    own_strips, high, low = pl.pallas_call(
        prepare_kernel,
        grid=(1,),
        in_specs=[whole(high), whole(low), whole(tile), whole(panel)],
        out_specs=[whole(panel), whole(high), whole(low)],
        out_shape=[jax.ShapeDtypeStruct((tiles, strip, NB), BF16), half_tile, half_tile],
        compiler_params=params,
        cost_estimate=pl.CostEstimate(flops=10 * NB**3, bytes_accessed=3 << 20, transcendentals=0),
    )(high, low, tile, panel)
    gathered = pltpu.with_memory_space_constraint(gathered, pltpu.HBM)
    trailing = pltpu.with_memory_space_constraint(trailing, pltpu.HBM)
    updated = pl.pallas_call(
        update_kernel,
        grid=(tiles,),
        in_specs=[
            whole(high),
            whole(low),
            pl.BlockSpec((cols_count, 1, strip, NB), lambda t: (0, t, 0, 0)),
            pl.BlockSpec((1, NB, NB), lambda t: (t, 0, 0)),
        ],
        out_specs=pl.BlockSpec((1, NB, NB), lambda t: (t, 0, 0)),
        out_shape=jax.ShapeDtypeStruct((tiles, NB, NB), BF16),
        compiler_params=params,
        cost_estimate=pl.CostEstimate(flops=16 * NB**3, bytes_accessed=6 << 20, transcendentals=0),
    )(high, low, gathered, trailing)

    return (
        own_factor.reshape(NB // rows_count, 1, NB // cols_count, 1),
        own_strips.reshape(tiles, 1, strip, NB),
        updated.reshape(tiles, 1, NB, 1, NB),
    )


def solution(mesh):
    in_specs = (P(None, "row", "col", None), P("row", "col"), P(None, "row", None, "col", None))
    out_specs = (
        P(None, "row", None, "col"),
        P(None, "row", "col", None),
        P(None, "row", None, "col", None),
    )
    return jax.shard_map(
        on_device, mesh=mesh, in_specs=in_specs, out_specs=out_specs, check_vma=False
    )
```
